32 devices in a mesh: replica: 16 (over z, y, x), shard: 2 (over core).
Axes of the slice: x: 2, y: 2, z: 4, core: 2. Of those that a mesh axis runs over, the one named last changes fastest.
Arguments:
- grad_query: float32 [32, 512, 384], P(('replica', 'shard')), may hold values from -0.3 to 0.3
- grad_output: float32 [32, 384, 512], P(('replica', 'shard')), may hold values from -0.3 to 0.3
- grad_norm: float32 [32, 512], P(('replica', 'shard')), may hold values from -0.3 to 0.3
- grad_bias: float32 [32, 32, 6], P(('replica', 'shard')), may hold values from -0.3 to 0.3
- weight_query: float32 [512, 384], P('shard'), may hold values from -5.303301 to 5.303301
- weight_output: float32 [384, 512], P('shard'), may hold values from -6.1237244 to 6.1237244
- weight_norm: float32 [512], P('shard'), may hold values from 0 to 120
- weight_bias: float32 [32, 6], P('shard'), may hold values from -120 to 120
- first_query: float32 [512, 384], P('shard'), may hold values from -120 to 120
- first_output: float32 [384, 512], P('shard'), may hold values from -120 to 120
- first_norm: float32 [512], P('shard'), may hold values from -120 to 120
- first_bias: float32 [32, 6], P('shard'), may hold values from -120 to 120
- second_query: float32 [512, 384], P('shard'), may hold values from 0.05 to 2
- second_output: float32 [384, 512], P('shard'), may hold values from 0.05 to 2
- second_norm: float32 [512], P('shard'), may hold values from 0.05 to 2
- second_bias: float32 [32, 6], P('shard'), may hold values from 0.05 to 2
Outputs:
- updated_query: bfloat16 [512, 384], replicated
- updated_output: bfloat16 [384, 512], replicated
- updated_norm: bfloat16 [512], replicated
- updated_bias: bfloat16 [32, 6], replicated
- first_query_next: float32 [512, 384], P('shard')
- first_output_next: float32 [384, 512], P('shard')
- first_norm_next: float32 [512], P('shard')
- first_bias_next: float32 [32, 6], P('shard')
- second_query_next: float32 [512, 384], P('shard')
- second_output_next: float32 [384, 512], P('shard')
- second_norm_next: float32 [512], P('shard')
- second_bias_next: float32 [32, 6], P('shard')
- norm_table: float32 [2, 4], replicated
- trust_ratios: float32 [4], replicated
The draws below stay inside these ranges and needn't reach their ends.
All inputs are finite; a program needn't handle non-finite values.
Results may differ from the reference program's by a relative error of at most 0.008.
Values may be sent and summed in bfloat16 or wider, within the bound.
A program may use at most 64 MiB of HBM per device.

```python
import math
import jax
import jax.numpy as jnp
from jax import lax

D = 512
HEADS = 6
BUCKETS = 32
INNER = 384
DEVICES = 32


def scaled_draw(key, row_count, column_count, factor, label):
    folded = jax.random.fold_in(key, label)
    subkeys = jax.random.split(folded, 3)
    row_scale = jnp.exp(jax.random.uniform(subkeys[1], (row_count, 1), jnp.float32) * math.log(10.0))
    column_scale = jnp.exp(jax.random.uniform(subkeys[2], (1, column_count), jnp.float32) * math.log(10.0))
    trend = jnp.exp(0.5 * math.log(3.0) * jnp.arange(row_count, dtype=jnp.float32) / row_count)[:, None]
    base = jax.random.normal(subkeys[0], (row_count, column_count), jnp.float32)
    base = jnp.clip(base, -4.0, 4.0)
    return base * row_scale * column_scale * trend * factor


def draw_weight_query(key, part):
    return scaled_draw(key, D, INNER, 0.1 / math.sqrt(D), 11)


def draw_weight_output(key, part):
    return scaled_draw(key, INNER, D, 0.1 / math.sqrt(INNER), 12)


def draw_weight_norm(key, part):
    return jnp.abs(scaled_draw(key, D, 1, 0.1, 13))[:, 0]


def draw_weight_bias(key, part):
    return scaled_draw(key, BUCKETS, HEADS, 0.1, 14)


def draw_first_query(key, part):
    return scaled_draw(key, D, INNER, 0.1, 15)


def draw_first_output(key, part):
    return scaled_draw(key, INNER, D, 0.1, 16)


def draw_first_norm(key, part):
    return scaled_draw(key, D, 1, 0.1, 17)[:, 0]


def draw_first_bias(key, part):
    return scaled_draw(key, BUCKETS, HEADS, 0.1, 18)


def strengthened(result, key, source, target, shards_of, factor):
    def block_of(dim):
        return (jnp.arange(result.shape[dim]) // (result.shape[dim] // shards_of)).reshape((-1,) + (1,) * (result.ndim - 1 - dim))

    one_side = jax.random.permutation(key, shards_of)[block_of(target)]
    other_side = (block_of(target) + shards_of // 2) % shards_of
    return jnp.where((block_of(source) == one_side) | (block_of(source) == other_side), factor * result, result)


def level_of(own_key, dims, pieces, smallest, top_value):
    gain, own = 1.0, jax.random.fold_in(own_key, 6)
    for dim, blocks in pieces:
        heights = jnp.exp(jax.random.uniform(jax.random.fold_in(own, dim), (blocks,), jnp.float32, smallest / len(pieces), top_value / len(pieces)))
        gain = gain * jnp.repeat(heights, dims[dim] // blocks).reshape([-1 if axis == dim else 1 for axis in range(len(dims))])
    return gain


def noise_with(own_key, shape, scale, bound, cuts, heavy, kind=jnp.bfloat16):
    values = scale * jax.random.normal(own_key, shape, jnp.float32)
    if cuts:
        values = values * level_of(own_key, shape, cuts, -0.22, 0.18)
    return jnp.clip(strengthened(values, jax.random.fold_in(own_key, 3), *heavy), -bound, bound).astype(kind)


def setup_inputs(seed: int = 0) -> dict:
    seeds = jax.random.split(jax.random.key(seed), 17)
    return {
        "grad_query": noise_with(seeds[0], (DEVICES, D, INNER), 0.05, 0.3, ((0, 32),), (0, 1, 32, 2.75), jnp.float32),
        "grad_output": noise_with(seeds[1], (DEVICES, INNER, D), 0.05, 0.3, ((0, 32),), (0, 1, 32, 2.75), jnp.float32),
        "grad_norm": noise_with(seeds[2], (DEVICES, D), 0.05, 0.3, ((0, 32),), (0, 1, 32, 2.75), jnp.float32),
        "grad_bias": noise_with(seeds[3], (DEVICES, BUCKETS, HEADS), 0.05, 0.3, ((0, 32),), (0, 1, 32, 2.75), jnp.float32),
        "weight_query": draw_weight_query(jax.random.fold_in(seeds[16], 71), 0),
        "weight_output": draw_weight_output(jax.random.fold_in(seeds[16], 71), 0),
        "weight_norm": draw_weight_norm(jax.random.fold_in(seeds[16], 71), 0),
        "weight_bias": draw_weight_bias(jax.random.fold_in(seeds[16], 71), 0),
        "first_query": draw_first_query(jax.random.fold_in(seeds[16], 71), 0),
        "first_output": draw_first_output(jax.random.fold_in(seeds[16], 71), 0),
        "first_norm": draw_first_norm(jax.random.fold_in(seeds[16], 71), 0),
        "first_bias": draw_first_bias(jax.random.fold_in(seeds[16], 71), 0),
        "second_query": jnp.clip(jnp.exp(math.log(2.0) - 3.6888794 * jax.random.uniform(seeds[12], (D, INNER), jnp.float32) ** level_of(seeds[12], (D, INNER), ((0, 2),), -0.2, 0.2)), 0.05, 2.0),
        "second_output": jnp.clip(jnp.exp(math.log(2.0) - 3.6888794 * jax.random.uniform(seeds[13], (INNER, D), jnp.float32) ** level_of(seeds[13], (INNER, D), ((0, 2),), -0.2, 0.2)), 0.05, 2.0),
        "second_norm": jnp.clip(jnp.exp(math.log(2.0) - 3.6888794 * jax.random.uniform(seeds[14], (D,), jnp.float32) ** level_of(seeds[14], (D,), ((0, 2),), -0.2, 0.2)), 0.05, 2.0),
        "second_bias": jnp.clip(jnp.exp(math.log(2.0) - 3.6888794 * jax.random.uniform(seeds[15], (BUCKETS, HEADS), jnp.float32) ** level_of(seeds[15], (BUCKETS, HEADS), ((0, 2),), -0.2, 0.2)), 0.05, 2.0),
    }


def lamb_piece(gradient, moment, second, weight, decay_rate):
    summed = lax.optimization_barrier(jnp.sum(gradient, axis=0))
    moment_next = 0.5 * moment + 0.5 * summed
    second_next = 0.5 * second + 0.5 * summed * summed
    update = moment_next / (jnp.sqrt(second_next) + 1e-06) + decay_rate * weight
    weight_size = jnp.sqrt(jnp.sum(weight * weight))
    update_size = jnp.sqrt(jnp.sum(update * update))
    ratio = weight_size / (update_size + 1e-06)
    updated = (weight - 0.01 * ratio * update).astype(jnp.bfloat16)
    return (updated, moment_next, second_next, weight_size, update_size, ratio)

def reference(grad_query, grad_output, grad_norm, grad_bias, weight_query, weight_output, weight_norm, weight_bias, first_query, first_output, first_norm, first_bias, second_query, second_output, second_norm, second_bias):
    query_out = lamb_piece(grad_query, first_query, second_query, weight_query, 0.01)
    output_out = lamb_piece(grad_output, first_output, second_output, weight_output, 0.01)
    norm_out = lamb_piece(grad_norm, first_norm, second_norm, weight_norm, 0.0)
    bias_out = lamb_piece(grad_bias, first_bias, second_bias, weight_bias, 0.0)
    listed = [query_out, output_out, norm_out, bias_out]
    weight_sizes = jnp.stack([entry[3] for entry in listed])
    update_sizes = jnp.stack([entry[4] for entry in listed])
    norm_table = jnp.stack([weight_sizes, update_sizes])
    trust_ratios = jnp.stack([entry[5] for entry in listed])
    return (query_out[0], output_out[0], norm_out[0], bias_out[0], query_out[1], output_out[1], norm_out[1], bias_out[1], query_out[2], output_out[2], norm_out[2], bias_out[2], norm_table, trust_ratios)
```

```python
import functools

import jax
import jax.numpy as jnp
from jax import lax
from jax.experimental import pallas as pl
from jax.experimental.pallas import tpu as pltpu
from jax.sharding import PartitionSpec as P

MESH = pl.DeviceIdType.MESH
LANES = 128
DECAY = 0.01


def up(value, step):
    return -(-value // step) * step


class Sizes:
    def __init__(self, shards, replicas, query, output, norm, bias):
        self.S, self.R = shards, replicas
        self.B = 4 if replicas % 4 == 0 else 1
        self.A = replicas // self.B
        self.n = (query[0], output[0])
        self.cols = (query[1], output[1])
        self.blocks = tuple(c // LANES for c in self.cols)
        self.used = tuple(n * j for n, j in zip(self.n, self.blocks))
        self.piece = tuple(up(-(-u // replicas), 16) for u in self.used)
        self.quarter = tuple(self.A * p for p in self.piece)
        self.total = tuple(replicas * p for p in self.piece)
        self.L = min(LANES, norm[0])
        self.q = norm[0] // self.L
        self.norm_rows = up(self.q * shards, 8)
        self.b, self.heads = bias
        self.small_rows = up(self.norm_rows + self.b * shards, 8)
        self.state_norm = up(3 * self.q, 8)
        self.bp = up(self.b, 8)
        self.state_rows = self.state_norm + 3 * self.bp


def step_math(summed, moment, second):
    moment_next = 0.5 * moment + 0.5 * summed
    second_next = 0.5 * second + 0.5 * summed * summed
    return moment_next, second_next, moment_next / (jnp.sqrt(second_next) + 1e-06)


def exchange_kernel(
    z,
    gq, go, gn, gb, wq, wo, wn, wb, fq, fo, fn, fb, sq, so, sn, sb,
    fin_q, fin_o, u_q, u_o, full_q, full_o, small_out, state, sums,
    core_q, core_o, acc_q, acc_o, send_q, send_o, plane_q, plane_o,
    quarter_q, quarter_o, zsend_q, zsend_o, zin_q, zin_o,
    wv_q, wv_o, fv_q, fv_o, sv_q, sv_o, small_core, small_plane, small_z,
    shard_send, shard_recv, plane_send, plane_recv, z_send, z_recv, local,
):
    S, B, A = z.S, z.B, z.A
    s = lax.axis_index("shard")
    r = lax.axis_index("replica")
    a, b = lax.div(r, B), lax.rem(r, B)
    grads, weights, firsts, seconds = (gq, go), (wq, wo), (fq, fo), (sq, so)
    fins, us, fulls = (fin_q, fin_o), (u_q, u_o), (full_q, full_o)
    cores, accs, sends, planes = (core_q, core_o), (acc_q, acc_o), (send_q, send_o), (plane_q, plane_o)
    quarters, zsends, zins = (quarter_q, quarter_o), (zsend_q, zsend_o), (zin_q, zin_o)
    wvs, fvs, svs = (wv_q, wv_o), (fv_q, fv_o), (sv_q, sv_o)
    started = []

    def shard_peer(d):
        return lax.rem(s + d, S)

    def plane_peer(d):
        return (a * B + lax.rem(b + d, B), s)

    def z_peer(d):
        return (lax.rem(a + d, A) * B + b, s)

    def go_to(src, dst, send, recv, device):
        copy = pltpu.make_async_remote_copy(
            src_ref=src, dst_ref=dst, send_sem=send, recv_sem=recv,
            device_id=device, device_id_type=MESH,
        )
        copy.start()
        started.append(copy)
        return copy

    def to_shard(kind, src_of, dst):
        return [
            go_to(src_of(shard_peer(d)), dst, shard_send.at[kind, d], shard_recv.at[kind, d], (r, shard_peer(d)))
            for d in range(1, S)
        ]

    def to_plane(kind, src_of, dst_of):
        return [
            go_to(src_of(lax.rem(b + d, B)), dst_of(d), plane_send.at[kind, d], plane_recv.at[kind, d], plane_peer(d))
            for d in range(1, B)
        ]

    def to_z(kind, src_of, dst_of):
        return [
            go_to(src_of(lax.rem(a + d, A)), dst_of(d), z_send.at[kind, d], z_recv.at[kind, d], z_peer(d))
            for d in range(1, A)
        ]

    def arrived(copies):
        for copy in copies:
            copy.wait_recv()

    def rows(index, count, step):
        return pl.ds(pl.multiple_of(index * count, step), count)

    own = []
    for c in range(2):
        copy = pltpu.make_async_copy(grads[c].at[0, rows(s, z.n[c], 8), :], cores[c].at[s], local.at[c])
        copy.start()
        own.append(copy)

    barrier = pltpu.get_barrier_semaphore()
    for d in range(1, S):
        pl.semaphore_signal(barrier, inc=1, device_id=(r, shard_peer(d)), device_id_type=MESH)
    for d in range(1, B):
        pl.semaphore_signal(barrier, inc=1, device_id=plane_peer(d), device_id_type=MESH)
    for d in range(1, A):
        pl.semaphore_signal(barrier, inc=1, device_id=z_peer(d), device_id_type=MESH)

    small_core[s] = jnp.zeros((z.small_rows, LANES), jnp.float32)
    for i in range(z.q * S):
        small_core[s, i : i + 1, : z.L] = gn[:, i * z.L : (i + 1) * z.L]
    small_core[s, z.norm_rows : z.norm_rows + z.b * S, : z.heads] = gb[0]
    state[s] = jnp.zeros((z.state_rows, LANES), jnp.float32)
    for t, ref in enumerate((wn, fn, sn)):
        for i in range(z.q):
            row = t * z.q + i
            state[s, row : row + 1, : z.L] = ref[:, i * z.L : (i + 1) * z.L]
    for t, ref in enumerate((wb, fb, sb)):
        row = z.state_norm + t * z.bp
        state[s, row : row + z.b, : z.heads] = ref[...]

    pl.semaphore_wait(barrier, S + B + A - 3)

    core_in = [
        to_shard(c, lambda peer, c=c: grads[c].at[0, rows(peer, z.n[c], 8), :], cores[c].at[s])
        for c in range(2)
    ]
    small_in = to_shard(2, lambda peer: small_core.at[s], small_core.at[s])
    held = []
    for c in range(2):
        for t, (src, dst) in enumerate(((weights[c], wvs[c]), (firsts[c], fvs[c]), (seconds[c], svs[c]))):
            copy = pltpu.make_async_copy(src, dst, local.at[2 + 3 * c + t])
            copy.start()
            held.append(copy)

    plane_in = []
    for c in range(2):
        own[c].wait()
        arrived(core_in[c])
        n = z.n[c]
        for j in range(z.blocks[c]):
            part = cores[c][0, :, j * LANES : (j + 1) * LANES]
            for k in range(1, S):
                part = part + cores[c][k, :, j * LANES : (j + 1) * LANES]
            accs[c][j * n : (j + 1) * n, :] = part
            sends[c][j * n : (j + 1) * n, :] = part.astype(jnp.bfloat16)
        if z.used[c] < z.total[c]:
            rest = (z.total[c] - z.used[c], LANES)
            accs[c][z.used[c] :, :] = jnp.zeros(rest, jnp.float32)
            sends[c][z.used[c] :, :] = jnp.zeros(rest, jnp.bfloat16)
        plane_in.append(
            to_plane(
                c,
                lambda peer, c=c: sends[c].at[rows(peer, z.quarter[c], 16), :],
                lambda d, c=c: planes[c].at[d - 1],
            )
        )
    arrived(small_in)
    small = small_core[0]
    for k in range(1, S):
        small = small + small_core[k]
    small_plane[b] = small
    small_in = to_plane(2, lambda peer: small_plane.at[b], lambda d: small_plane.at[b])

    late = []
    for c in range(2):
        late += to_shard(3 + c, lambda peer, c=c: weights[c], fulls[c].at[rows(s, z.n[c], 8), :])
        copy = pltpu.make_async_copy(weights[c], fulls[c].at[rows(s, z.n[c], 8), :], local.at[8 + c])
        copy.start()
        held.append(copy)
    late += to_shard(5, lambda peer: state.at[s], state.at[s])

    z_in = []
    for c in range(2):
        arrived(plane_in[c])
        part = accs[c][rows(b, z.quarter[c], 16), :]
        for d in range(1, B):
            part = part + planes[c][d - 1].astype(jnp.float32)
        quarters[c][...] = part
        zsends[c][...] = part.astype(jnp.bfloat16)
        z_in.append(
            to_z(
                c,
                lambda peer, c=c: zsends[c].at[rows(peer, z.piece[c], 16), :],
                lambda d, c=c: zins[c].at[d - 1],
            )
        )
    arrived(small_in)
    small = small_plane[0]
    for k in range(1, B):
        small = small + small_plane[k]
    small_z[a] = small
    small_in = to_z(2, lambda peer: small_z.at[a], lambda d: small_z.at[a])

    back_z = []
    for c in range(2):
        arrived(z_in[c])
        part = quarters[c][rows(a, z.piece[c], 16), :]
        for d in range(1, A):
            part = part + zins[c][d - 1].astype(jnp.float32)
        mine = rows(b * A + a, z.piece[c], 16)
        fins[c][mine, :] = part.astype(jnp.bfloat16)
        back_z.append(
            to_z(3 + c, lambda peer, c=c, mine=mine: fins[c].at[mine, :], lambda d, c=c, mine=mine: fins[c].at[mine, :])
        )

    back_plane = []
    for c in range(2):
        arrived(back_z[c])
        mine = rows(b, z.quarter[c], 16)
        back_plane.append(
            to_plane(3 + c, lambda peer, c=c, mine=mine: fins[c].at[mine, :], lambda d, c=c, mine=mine: fins[c].at[mine, :])
        )
    arrived(small_in)
    small = small_z[0]
    for k in range(1, A):
        small = small + small_z[k]
    small_out[...] = small
    for copy in held:
        copy.wait()
    sums[s] = jnp.zeros((8, LANES), jnp.float32)
    for c in range(2):
        squares = jnp.zeros((1, LANES), jnp.float32)
        for j in range(z.blocks[c]):
            weight = wvs[c][:, j * LANES : (j + 1) * LANES]
            squares = squares + jnp.sum(weight * weight, axis=0, keepdims=True)
        sums[s, 2 * c : 2 * c + 1, :] = squares

    for c in range(2):
        arrived(back_plane[c])
        n = z.n[c]
        mine = rows(s, n, 16)
        squares = jnp.zeros((1, LANES), jnp.float32)
        for j in range(z.blocks[c]):
            lanes = slice(j * LANES, (j + 1) * LANES)
            summed = fins[c][j * n : (j + 1) * n, :].astype(jnp.float32)
            _, _, update = step_math(summed, fvs[c][:, lanes], svs[c][:, lanes])
            update = update + DECAY * wvs[c][:, lanes]
            squares = squares + jnp.sum(update * update, axis=0, keepdims=True)
            us[c][mine, lanes] = update.astype(jnp.bfloat16)
        sums[s, 2 * c + 1 : 2 * c + 2, :] = squares
        late += to_shard(6 + c, lambda peer, c=c, mine=mine: us[c].at[mine, :], us[c].at[mine, :])
    late += to_shard(8, lambda peer: sums.at[s], sums.at[s])
    arrived(late)
    for copy in started:
        copy.wait_send()


def finish_kernel(
    z,
    fin_q, fin_o, u_q, u_o, full_q, full_o, small, state, sums, fq, fo, sq, so,
    new_q, new_o, new_n, new_b, fq_next, fo_next, fn_next, fb_next,
    sq_next, so_next, sn_next, sb_next, table, trust,
):
    S, L, h = z.S, z.L, z.heads
    s = lax.axis_index("shard")
    totals = sums[0]
    for k in range(1, S):
        totals = totals + sums[k]

    def whole(row):
        return jnp.sum(totals[row : row + 1, :], axis=1, keepdims=True)

    squares = [(whole(0), whole(1)), (whole(2), whole(3))]

    def norm_of(k):
        rows = [state[k, t * z.q : (t + 1) * z.q, :L] for t in range(3)]
        return small[pl.ds(k * z.q, z.q), :L], rows

    def bias_of(k):
        rows = [state[k, z.state_norm + t * z.bp : z.state_norm + t * z.bp + z.b, :h] for t in range(3)]
        return small[pl.ds(z.norm_rows + k * z.b, z.b), :h], rows

    def total(value):
        return jnp.sum(jnp.sum(value, axis=0, keepdims=True), axis=1, keepdims=True)

    pairs = []
    for part_of in (norm_of, bias_of):
        couples, wsum, usum = [], None, None
        for k in range(S):
            summed, (weight, moment, second) = part_of(k)
            update = step_math(summed, moment, second)[2]
            couples.append((weight, update))
            ws, us = total(weight * weight), total(update * update)
            wsum = ws if wsum is None else wsum + ws
            usum = us if usum is None else usum + us
        squares.append((wsum, usum))
        pairs.append(couples)

    wsizes = [jnp.sqrt(pair[0]) for pair in squares]
    usizes = [jnp.sqrt(pair[1]) for pair in squares]
    ratios = [w / (u + 1e-06) for w, u in zip(wsizes, usizes)]

    column = lax.broadcasted_iota(jnp.int32, (2, 4), 1)
    row = lax.broadcasted_iota(jnp.int32, (2, 4), 0)
    values = jnp.zeros((2, 4), jnp.float32)
    for k in range(4):
        values = jnp.where(column == k, jnp.where(row == 0, wsizes[k], usizes[k]), values)
    table[...] = values
    column = lax.broadcasted_iota(jnp.int32, (1, 4), 1)
    values = jnp.zeros((1, 4), jnp.float32)
    for k in range(4):
        values = jnp.where(column == k, ratios[k], values)
    trust[...] = values

    for k in range(S):
        weight, update = pairs[0][k]
        value = (weight - 0.01 * ratios[2] * update).astype(jnp.bfloat16)
        for i in range(z.q):
            at = (k * z.q + i) * L
            new_n[:, at : at + L] = value[i : i + 1, :]
        weight, update = pairs[1][k]
        new_b[k * z.b : (k + 1) * z.b, :] = (weight - 0.01 * ratios[3] * update).astype(jnp.bfloat16)
    summed, (_, moment, second) = norm_of(s)
    moment_next, second_next, _ = step_math(summed, moment, second)
    for i in range(z.q):
        fn_next[:, i * L : (i + 1) * L] = moment_next[i : i + 1, :]
        sn_next[:, i * L : (i + 1) * L] = second_next[i : i + 1, :]
    summed, (_, moment, second) = bias_of(s)
    moment_next, second_next, _ = step_math(summed, moment, second)
    fb_next[...] = moment_next
    sb_next[...] = second_next

    for c, (fin, u, full, first, second, new, first_next, second_next) in enumerate((
        (fin_q, u_q, full_q, fq, sq, new_q, fq_next, sq_next),
        (fin_o, u_o, full_o, fo, so, new_o, fo_next, so_next),
    )):
        n = z.n[c]
        for j in range(z.blocks[c]):
            lanes = slice(j * LANES, (j + 1) * LANES)
            summed = fin[j * n : (j + 1) * n, :].astype(jnp.float32)
            moment_value, second_value, _ = step_math(summed, first[:, lanes], second[:, lanes])
            first_next[:, lanes] = moment_value
            second_next[:, lanes] = second_value
        new[...] = (full[...] - 0.01 * ratios[c] * u[...].astype(jnp.float32)).astype(jnp.bfloat16)


def on_device(
    shards, replicas,
    gq, go, gn, gb, wq, wo, wn, wb, fq, fo, fn, fb, sq, so, sn, sb,
):
    f32, bf16 = jnp.float32, jnp.bfloat16
    z = Sizes(shards, replicas, wq.shape, wo.shape, wn.shape, wb.shape)
    S, B, A = z.S, z.B, z.A
    wn, fn, sn = (value.reshape(1, -1) for value in (wn, fn, sn))
    any_spec = pl.BlockSpec(memory_space=pl.ANY)
    vmem = pl.BlockSpec(memory_space=pltpu.VMEM)
    shape = jax.ShapeDtypeStruct
    whole = [(n * S, cols) for n, cols in zip(z.n, z.cols)]
    both = (0, 1)

    def scratch(shape_of, dtype):
        return [pltpu.VMEM(shape_of(c), dtype) for c in both]

    outs = pl.pallas_call(
        functools.partial(exchange_kernel, z),
        out_shape=[shape((z.total[c], LANES), bf16) for c in both]
        + [shape(whole[c], bf16) for c in both]
        + [shape(whole[c], f32) for c in both]
        + [shape((z.small_rows, LANES), f32), shape((S, z.state_rows, LANES), f32), shape((S, 8, LANES), f32)],
        in_specs=[any_spec, any_spec, vmem, vmem] + [any_spec, any_spec, vmem, vmem] * 3,
        out_specs=[vmem] * 4 + [any_spec] * 2 + [vmem] * 3,
        scratch_shapes=scratch(lambda c: (S, z.n[c], z.cols[c]), f32)
        + scratch(lambda c: (z.total[c], LANES), f32)
        + scratch(lambda c: (z.total[c], LANES), bf16)
        + scratch(lambda c: (max(B - 1, 1), z.quarter[c], LANES), bf16)
        + scratch(lambda c: (z.quarter[c], LANES), f32)
        + scratch(lambda c: (z.quarter[c], LANES), bf16)
        + scratch(lambda c: (max(A - 1, 1), z.piece[c], LANES), bf16)
        + scratch(lambda c: (z.n[c], z.cols[c]), f32) * 3
        + [pltpu.VMEM((k, z.small_rows, LANES), f32) for k in (S, B, A)]
        + [pltpu.SemaphoreType.DMA((9, S))] * 2
        + [pltpu.SemaphoreType.DMA((5, B))] * 2
        + [pltpu.SemaphoreType.DMA((5, A))] * 2
        + [pltpu.SemaphoreType.DMA((10,))],
        compiler_params=pltpu.CompilerParams(
            collective_id=0, has_side_effects=True, vmem_limit_bytes=40 * 1024 * 1024
        ),
        name="exchange",
    )(gq, go, gn, gb, wq, wo, wn, wb, fq, fo, fn, fb, sq, so, sn, sb)

    results = pl.pallas_call(
        functools.partial(finish_kernel, z),
        out_shape=[
            shape(whole[0], bf16), shape(whole[1], bf16),
            shape((1, wn.shape[1] * S), bf16), shape((z.b * S, z.heads), bf16),
        ]
        + [shape(ref.shape, f32) for ref in (fq, fo, fn, fb)] * 2
        + [shape((2, 4), f32), shape((1, 4), f32)],
        in_specs=[vmem] * 13,
        out_specs=[vmem] * 14,
        compiler_params=pltpu.CompilerParams(vmem_limit_bytes=40 * 1024 * 1024),
        name="finish",
    )(*outs, fq, fo, sq, so)
    results = list(results)
    for at in (2, 6, 10, 13):
        results[at] = results[at].reshape(-1)
    return tuple(results)


def solution(mesh):
    shards, replicas = mesh.shape["shard"], mesh.shape["replica"]
    every = ("replica", "shard")
    state = (P("shard", None), P("shard", None), P("shard"), P("shard", None))
    return jax.shard_map(
        functools.partial(on_device, shards, replicas),
        mesh=mesh,
        in_specs=(P(every, None, None), P(every, None, None), P(every, None), P(every, None, None)) + state * 3,
        out_specs=(P(), P(), P(), P()) + state * 2 + (P(), P()),
        check_vma=False,
    )
```

```python
import functools

import jax
import jax.numpy as jnp
from jax import lax
from jax.experimental import pallas as pl
from jax.experimental.pallas import tpu as pltpu
from jax.sharding import PartitionSpec as P

MESH = pl.DeviceIdType.MESH
LANES = 128
DECAY = 0.01


def up(value, step):
    return -(-value // step) * step


class Sizes:
    def __init__(self, shards, replicas, query, output, norm, bias):
        self.S, self.R = shards, replicas
        self.B = 4 if replicas % 4 == 0 else 1
        self.A = replicas // self.B
        self.n = (query[0], output[0])
        self.cols = (query[1], output[1])
        self.blocks = tuple(c // LANES for c in self.cols)
        self.used = tuple(n * j for n, j in zip(self.n, self.blocks))
        self.piece = tuple(up(-(-u // replicas), 16) for u in self.used)
        self.quarter = tuple(self.A * p for p in self.piece)
        self.total = tuple(replicas * p for p in self.piece)
        self.L = min(LANES, norm[0])
        self.q = norm[0] // self.L
        self.norm_rows = up(self.q * shards, 8)
        self.heads, self.b = bias
        self.hp = up(self.heads, 8)
        self.small_rows = self.norm_rows + self.hp
        self.state_norm = up(3 * self.q, 8)
        self.state_rows = self.state_norm + 3 * self.hp
        self.sum_rows = up(2 * (self.B + 1), 8)


def step_math(summed, moment, second):
    moment_next = 0.5 * moment + 0.5 * summed
    second_next = 0.5 * second + 0.5 * summed * summed
    return moment_next, second_next, moment_next / (jnp.sqrt(second_next) + 1e-06)


def exchange_kernel(
    z,
    gq, go, gn_h, gb_h, wq, wo, wn_h, wb_h, fq, fo, fn_h, fb_h, sq, so, sn_h, sb_h,
    fin_q, fin_o, u_q, u_o, full_q, full_o, small_out, state, sums,
    core_q, core_o, acc_q, acc_o, send_q, send_o, plane_q, plane_o,
    quarter_q, quarter_o, zsend_q, zsend_o, zin_q, zin_o,
    wv_q, wv_o, fv_q, fv_o, sv_q, sv_o, small_core, small_plane, small_z,
    gn, gb, wn, wb, fn, fb, sn, sb,
    shard_send, shard_recv, plane_send, plane_recv, z_send, z_recv, local, packing,
):
    S, B, A = z.S, z.B, z.A
    s = lax.axis_index("shard")
    r = lax.axis_index("replica")
    a, b = lax.div(r, B), lax.rem(r, B)
    grads, weights, firsts, seconds = (gq, go), (wq, wo), (fq, fo), (sq, so)
    fins, us, fulls = (fin_q, fin_o), (u_q, u_o), (full_q, full_o)
    cores, accs, sends, planes = (core_q, core_o), (acc_q, acc_o), (send_q, send_o), (plane_q, plane_o)
    quarters, zsends, zins = (quarter_q, quarter_o), (zsend_q, zsend_o), (zin_q, zin_o)
    wvs, fvs, svs = (wv_q, wv_o), (fv_q, fv_o), (sv_q, sv_o)
    started = []

    def shard_peer(d):
        return lax.rem(s + d, S)

    def plane_peer(d):
        return (a * B + lax.rem(b + d, B), s)

    def z_peer(d):
        return (lax.rem(a + d, A) * B + b, s)

    def go_to(src, dst, send, recv, device):
        copy = pltpu.make_async_remote_copy(
            src_ref=src, dst_ref=dst, send_sem=send, recv_sem=recv,
            device_id=device, device_id_type=MESH,
        )
        copy.start()
        started.append(copy)
        return copy

    def to_shard(kind, src_of, dst):
        return [
            go_to(src_of(shard_peer(d)), dst, shard_send.at[kind, d], shard_recv.at[kind, d], (r, shard_peer(d)))
            for d in range(1, S)
        ]

    def to_plane(kind, src_of, dst_of):
        return [
            go_to(src_of(lax.rem(b + d, B)), dst_of(d), plane_send.at[kind, d], plane_recv.at[kind, d], plane_peer(d))
            for d in range(1, B)
        ]

    def to_z(kind, src_of, dst_of):
        return [
            go_to(src_of(lax.rem(a + d, A)), dst_of(d), z_send.at[kind, d], z_recv.at[kind, d], z_peer(d))
            for d in range(1, A)
        ]

    def arrived(copies):
        for copy in copies:
            copy.wait_recv()

    def rows(index, count, step):
        return pl.ds(pl.multiple_of(index * count, step), count)

    own = []
    for c in range(2):
        copy = pltpu.make_async_copy(grads[c].at[0, rows(s, z.n[c], 8), :], cores[c].at[s], local.at[c])
        copy.start()
        own.append(copy)

    tiny = []
    for i, (src, dst) in enumerate((
        (gn_h, gn), (gb_h, gb), (wn_h, wn), (wb_h, wb), (fn_h, fn), (fb_h, fb), (sn_h, sn), (sb_h, sb),
    )):
        copy = pltpu.make_async_copy(src, dst, local.at[2 + i])
        copy.start()
        tiny.append(copy)

    barrier = pltpu.get_barrier_semaphore()
    for d in range(1, S):
        pl.semaphore_signal(barrier, inc=1, device_id=(r, shard_peer(d)), device_id_type=MESH)
    for d in range(1, B):
        pl.semaphore_signal(barrier, inc=1, device_id=plane_peer(d), device_id_type=MESH)
    for d in range(1, A):
        pl.semaphore_signal(barrier, inc=1, device_id=z_peer(d), device_id_type=MESH)

    pl.semaphore_wait(barrier, S + B + A - 3)

    core_in = [
        to_shard(c, lambda peer, c=c: grads[c].at[0, rows(peer, z.n[c], 8), :], cores[c].at[s])
        for c in range(2)
    ]

    for copy in tiny:
        copy.wait()
    small_core[s] = jnp.zeros((z.small_rows, LANES), jnp.float32)
    for i in range(z.q * S):
        small_core[s, i : i + 1, : z.L] = gn[:, i * z.L : (i + 1) * z.L]
    for h in range(z.heads):
        small_core[s, z.norm_rows + h : z.norm_rows + h + 1, : z.b * S] = gb[h]
    state[s] = jnp.zeros((z.state_rows, LANES), jnp.float32)
    for t, ref in enumerate((wn, fn, sn)):
        for i in range(z.q):
            row = t * z.q + i
            state[s, row : row + 1, : z.L] = ref[:, i * z.L : (i + 1) * z.L]
    for t, ref in enumerate((wb, fb, sb)):
        row = z.state_norm + t * z.hp
        state[s, row : row + z.heads, : z.b] = ref[...]
    small_in = to_shard(2, lambda peer: small_core.at[s], small_core.at[s])

    held = []
    for c in range(2):
        n = z.n[c]
        for t, (src, dst) in enumerate(((weights[c], wvs[c]), (firsts[c], fvs[c]), (seconds[c], svs[c]))):
            for j in range(z.blocks[c]):
                copy = pltpu.make_async_copy(
                    src.at[:, j * LANES : (j + 1) * LANES], dst.at[j * n : (j + 1) * n, :], packing.at[3 * c + t, j]
                )
                copy.start()
                held.append(copy)
            if z.used[c] < z.total[c]:
                dst[z.used[c] :, :] = jnp.zeros((z.total[c] - z.used[c], LANES), jnp.float32)

    plane_in = []
    for c in range(2):
        own[c].wait()
        arrived(core_in[c])
        n = z.n[c]
        for j in range(z.blocks[c]):
            part = cores[c][0, :, j * LANES : (j + 1) * LANES]
            for k in range(1, S):
                part = part + cores[c][k, :, j * LANES : (j + 1) * LANES]
            accs[c][j * n : (j + 1) * n, :] = part
            sends[c][j * n : (j + 1) * n, :] = part.astype(jnp.bfloat16)
        if z.used[c] < z.total[c]:
            rest = (z.total[c] - z.used[c], LANES)
            accs[c][z.used[c] :, :] = jnp.zeros(rest, jnp.float32)
            sends[c][z.used[c] :, :] = jnp.zeros(rest, jnp.bfloat16)
        plane_in.append(
            to_plane(
                c,
                lambda peer, c=c: sends[c].at[rows(peer, z.quarter[c], 16), :],
                lambda d, c=c: planes[c].at[d - 1],
            )
        )
    arrived(small_in)
    small = small_core[0]
    for k in range(1, S):
        small = small + small_core[k]
    small_plane[b] = small
    small_in = to_plane(2, lambda peer: small_plane.at[b], lambda d: small_plane.at[b])

    late = []
    for c in range(2):
        late += to_shard(3 + c, lambda peer, c=c: weights[c], fulls[c].at[rows(s, z.n[c], 8), :])
        copy = pltpu.make_async_copy(weights[c], fulls[c].at[rows(s, z.n[c], 8), :], local.at[10 + c])
        copy.start()
        held.append(copy)
    late += to_shard(5, lambda peer: state.at[s], state.at[s])

    z_in = []
    for c in range(2):
        arrived(plane_in[c])
        part = accs[c][rows(b, z.quarter[c], 16), :]
        for d in range(1, B):
            part = part + planes[c][d - 1].astype(jnp.float32)
        quarters[c][...] = part
        zsends[c][...] = part.astype(jnp.bfloat16)
        z_in.append(
            to_z(
                c,
                lambda peer, c=c: zsends[c].at[rows(peer, z.piece[c], 16), :],
                lambda d, c=c: zins[c].at[d - 1],
            )
        )
    arrived(small_in)
    small = small_plane[0]
    for k in range(1, B):
        small = small + small_plane[k]
    small_z[a] = small
    small_in = to_z(2, lambda peer: small_z.at[a], lambda d: small_z.at[a])

    back_z = []
    for c in range(2):
        arrived(z_in[c])
        part = quarters[c][rows(a, z.piece[c], 16), :]
        for d in range(1, A):
            part = part + zins[c][d - 1].astype(jnp.float32)
        mine = rows(b * A + a, z.piece[c], 16)
        fins[c][mine, :] = part.astype(jnp.bfloat16)
        back_z.append(
            to_z(3 + c, lambda peer, c=c, mine=mine: fins[c].at[mine, :], lambda d, c=c, mine=mine: fins[c].at[mine, :])
        )

    back_plane = []
    for c in range(2):
        arrived(back_z[c])
        mine = rows(b, z.quarter[c], 16)
        back_plane.append(
            to_plane(3 + c, lambda peer, c=c, mine=mine: fins[c].at[mine, :], lambda d, c=c, mine=mine: fins[c].at[mine, :])
        )
    for copy in held:
        copy.wait()
    sums[s] = jnp.zeros((z.sum_rows, LANES), jnp.float32)
    for c in range(2):
        weight = wvs[c][...]
        sums[s, c * (B + 1) : c * (B + 1) + 1, :] = jnp.sum(weight * weight, axis=0, keepdims=True)

    def updates(c, d):
        index = lax.rem(b + B - d, B)
        mine = rows(index, z.quarter[c], 16)
        summed = fins[c][mine, :].astype(jnp.float32)
        _, _, update = step_math(summed, fvs[c][mine, :], svs[c][mine, :])
        update = update + DECAY * wvs[c][mine, :]
        sums[s, pl.ds(c * (B + 1) + 1 + index, 1), :] = jnp.sum(update * update, axis=0, keepdims=True)
        us[c][s, mine, :] = update.astype(jnp.bfloat16)
        return to_shard(
            6 + c * B + d, lambda peer: us[c].at[s, mine, :], us[c].at[s, mine, :]
        )

    for c in range(2):
        late += updates(c, 0)
    arrived(small_in)
    small = small_z[0]
    for k in range(1, A):
        small = small + small_z[k]
    small_out[...] = small
    for c in range(2):
        for d in range(1, B):
            back_plane[c][d - 1].wait_recv()
            late += updates(c, d)
    late += to_shard(6 + 2 * B, lambda peer: sums.at[s], sums.at[s])
    arrived(late)
    for copy in started:
        copy.wait_send()


def finish_kernel(
    z,
    fin_q, fin_o, u_q, u_o, full_q, full_o, small, state, sums, fq, fo, sq, so,
    new_q, new_o, new_n, new_b, fq_next, fo_next, fn_next, fb_next,
    sq_next, so_next, sn_next, sb_next, table, trust,
):
    S, L, h = z.S, z.L, z.heads
    s = lax.axis_index("shard")
    totals = sums[0]
    for k in range(1, S):
        totals = totals + sums[k]

    def whole(row, count):
        value = totals[row : row + 1, :]
        for i in range(1, count):
            value = value + totals[row + i : row + i + 1, :]
        return jnp.sum(value, axis=1, keepdims=True)

    squares = [(whole(c * (z.B + 1), 1), whole(c * (z.B + 1) + 1, z.B)) for c in range(2)]

    def norm_of(k):
        rows = [state[k, t * z.q : (t + 1) * z.q, :L] for t in range(3)]
        return small[pl.ds(k * z.q, z.q), :L], rows

    def bias_of(k):
        rows = [state[k, z.state_norm + t * z.hp : z.state_norm + t * z.hp + h, : z.b] for t in range(3)]
        return small[z.norm_rows : z.norm_rows + h, k * z.b : (k + 1) * z.b], rows

    def total(value):
        return jnp.sum(jnp.sum(value, axis=0, keepdims=True), axis=1, keepdims=True)

    pairs = []
    for part_of in (norm_of, bias_of):
        couples, wsum, usum = [], None, None
        for k in range(S):
            summed, (weight, moment, second) = part_of(k)
            update = step_math(summed, moment, second)[2]
            couples.append((weight, update))
            ws, us = total(weight * weight), total(update * update)
            wsum = ws if wsum is None else wsum + ws
            usum = us if usum is None else usum + us
        squares.append((wsum, usum))
        pairs.append(couples)

    wsizes = [jnp.sqrt(pair[0]) for pair in squares]
    usizes = [jnp.sqrt(pair[1]) for pair in squares]
    ratios = [w / (u + 1e-06) for w, u in zip(wsizes, usizes)]

    column = lax.broadcasted_iota(jnp.int32, (2, 4), 1)
    row = lax.broadcasted_iota(jnp.int32, (2, 4), 0)
    values = jnp.zeros((2, 4), jnp.float32)
    for k in range(4):
        values = jnp.where(column == k, jnp.where(row == 0, wsizes[k], usizes[k]), values)
    table[...] = values
    column = lax.broadcasted_iota(jnp.int32, (1, 4), 1)
    values = jnp.zeros((1, 4), jnp.float32)
    for k in range(4):
        values = jnp.where(column == k, ratios[k], values)
    trust[...] = values

    for k in range(S):
        weight, update = pairs[0][k]
        value = (weight - 0.01 * ratios[2] * update).astype(jnp.bfloat16)
        for i in range(z.q):
            at = (k * z.q + i) * L
            new_n[at : at + L] = value[i]
        weight, update = pairs[1][k]
        new_b[:, k * z.b : (k + 1) * z.b] = (weight - 0.01 * ratios[3] * update).astype(jnp.bfloat16)
    summed, (_, moment, second) = norm_of(s)
    moment_next, second_next, _ = step_math(summed, moment, second)
    for i in range(z.q):
        fn_next[:, i * L : (i + 1) * L] = moment_next[i : i + 1, :]
        sn_next[:, i * L : (i + 1) * L] = second_next[i : i + 1, :]
    moment_next = second_next = jnp.zeros((h, z.b), jnp.float32)
    for k in range(S):
        summed, (_, moment, second) = bias_of(k)
        moment_value, second_value, _ = step_math(summed, moment, second)
        moment_next = jnp.where(s == k, moment_value, moment_next)
        second_next = jnp.where(s == k, second_value, second_next)
    fb_next[...] = moment_next
    sb_next[...] = second_next

    for c, (fin, u, full, first, second, new, first_next, second_next) in enumerate((
        (fin_q, u_q, full_q, fq, sq, new_q, fq_next, sq_next),
        (fin_o, u_o, full_o, fo, so, new_o, fo_next, so_next),
    )):
        n = z.n[c]
        for j in range(z.blocks[c]):
            lanes = slice(j * LANES, (j + 1) * LANES)
            summed = fin[j * n : (j + 1) * n, :].astype(jnp.float32)
            moment_value, second_value, _ = step_math(summed, first[:, lanes], second[:, lanes])
            first_next[:, lanes] = moment_value
            second_next[:, lanes] = second_value
            for k in range(S):
                own = slice(k * n, (k + 1) * n)
                update = u[k, j * n : (j + 1) * n, :].astype(jnp.float32)
                new[own, lanes] = (full[own, lanes] - 0.01 * ratios[c] * update).astype(jnp.bfloat16)


def on_device(
    shards, replicas,
    gq, go, gn, gb, wq, wo, wn, wb, fq, fo, fn, fb, sq, so, sn, sb,
):
    f32, bf16 = jnp.float32, jnp.bfloat16
    wb, fb, sb = (value.T for value in (wb, fb, sb))
    gb = jnp.transpose(gb, (2, 0, 1))
    z = Sizes(shards, replicas, wq.shape, wo.shape, wn.shape, wb.shape)
    S, B, A = z.S, z.B, z.A
    wn, fn, sn = (value.reshape(1, -1) for value in (wn, fn, sn))
    any_spec = pl.BlockSpec(memory_space=pl.ANY)
    vmem = pl.BlockSpec(memory_space=pltpu.VMEM)
    shape = jax.ShapeDtypeStruct
    whole = [(n * S, cols) for n, cols in zip(z.n, z.cols)]
    both = (0, 1)

    def scratch(shape_of, dtype):
        return [pltpu.VMEM(shape_of(c), dtype) for c in both]

    outs = pl.pallas_call(
        functools.partial(exchange_kernel, z),
        out_shape=[shape((z.total[c], LANES), bf16) for c in both]
        + [shape((S, z.total[c], LANES), bf16) for c in both]
        + [shape(whole[c], f32) for c in both]
        + [shape((z.small_rows, LANES), f32), shape((S, z.state_rows, LANES), f32), shape((S, z.sum_rows, LANES), f32)],
        in_specs=[pl.BlockSpec(memory_space=pltpu.HBM)] * 16,
        out_specs=[vmem] * 4 + [any_spec] * 2 + [vmem] * 3,
        scratch_shapes=scratch(lambda c: (S, z.n[c], z.cols[c]), f32)
        + scratch(lambda c: (z.total[c], LANES), f32)
        + scratch(lambda c: (z.total[c], LANES), bf16)
        + scratch(lambda c: (max(B - 1, 1), z.quarter[c], LANES), bf16)
        + scratch(lambda c: (z.quarter[c], LANES), f32)
        + scratch(lambda c: (z.quarter[c], LANES), bf16)
        + scratch(lambda c: (max(A - 1, 1), z.piece[c], LANES), bf16)
        + scratch(lambda c: (z.total[c], LANES), f32) * 3
        + [pltpu.VMEM((k, z.small_rows, LANES), f32) for k in (S, B, A)]
        + [pltpu.VMEM(value.shape, f32) for value in (gn, gb, wn, wb, fn, fb, sn, sb)]
        + [pltpu.SemaphoreType.DMA((7 + 2 * B, S))] * 2
        + [pltpu.SemaphoreType.DMA((5, B))] * 2
        + [pltpu.SemaphoreType.DMA((5, A))] * 2
        + [pltpu.SemaphoreType.DMA((12,)), pltpu.SemaphoreType.DMA((6, max(z.blocks)))],
        compiler_params=pltpu.CompilerParams(
            collective_id=0, has_side_effects=True, vmem_limit_bytes=60 * 1024 * 1024
        ),
        name="exchange",
    )(gq, go, gn, gb, wq, wo, wn, wb, fq, fo, fn, fb, sq, so, sn, sb)

    results = pl.pallas_call(
        functools.partial(finish_kernel, z),
        out_shape=[
            shape(whole[0], bf16), shape(whole[1], bf16),
            shape((wn.shape[1] * S,), bf16), shape((z.heads, z.b * S), bf16),
        ]
        + [shape(ref.shape, f32) for ref in (fq, fo, fn, fb)] * 2
        + [shape((2, 4), f32), shape((1, 4), f32)],
        in_specs=[vmem] * 13,
        out_specs=[vmem] * 14,
        compiler_params=pltpu.CompilerParams(vmem_limit_bytes=40 * 1024 * 1024),
        name="finish",
    )(*outs, fq, fo, sq, so)
    results = list(results)
    for at in (6, 10, 13):
        results[at] = results[at].reshape(-1)
    for at in (3, 7, 11):
        results[at] = results[at].T
    return tuple(results)


def solution(mesh):
    shards, replicas = mesh.shape["shard"], mesh.shape["replica"]
    every = ("replica", "shard")
    state = (P("shard", None), P("shard", None), P("shard"), P("shard", None))
    return jax.shard_map(
        functools.partial(on_device, shards, replicas),
        mesh=mesh,
        in_specs=(P(every, None, None), P(every, None, None), P(every, None), P(every, None, None)) + state * 3,
        out_specs=(P(), P(), P(), P()) + state * 2 + (P(), P()),
        check_vma=False,
    )
```

```python
import functools

import jax
import jax.numpy as jnp
from jax import lax
from jax.experimental import pallas as pl
from jax.experimental.pallas import tpu as pltpu
from jax.sharding import PartitionSpec as P

MESH = pl.DeviceIdType.MESH
LANES = 128
DECAY = 0.01


def up(value, step):
    return -(-value // step) * step


class Sizes:
    def __init__(self, shards, replicas, query, output, norm, bias):
        self.S, self.R = shards, replicas
        self.B = 4 if replicas % 4 == 0 else 1
        self.A = replicas // self.B
        self.n = (query[0], output[0])
        self.cols = (query[1], output[1])
        self.blocks = tuple(c // LANES for c in self.cols)
        self.used = tuple(n * j for n, j in zip(self.n, self.blocks))
        self.piece = tuple(up(-(-u // replicas), 16) for u in self.used)
        self.quarter = tuple(self.A * p for p in self.piece)
        self.total = tuple(replicas * p for p in self.piece)
        self.L = min(LANES, norm[0])
        self.q = norm[0] // self.L
        self.norm_rows = up(self.q * shards, 8)
        self.heads, self.b = bias
        self.hp = up(self.heads, 8)
        self.small_rows = self.norm_rows + self.hp
        self.state_norm = up(3 * self.q, 8)
        self.state_rows = self.state_norm + 3 * self.hp
        self.sum_rows = up(2 * (self.B + 1), 8)


def step_math(summed, moment, second):
    moment_next = 0.5 * moment + 0.5 * summed
    second_next = 0.5 * second + 0.5 * summed * summed
    return moment_next, second_next, moment_next / (jnp.sqrt(second_next) + 1e-06)


def exchange_kernel(
    z,
    gq, go, gn_h, gb_h, wq, wo, wn_h, wb_h, fq, fo, fn_h, fb_h, sq, so, sn_h, sb_h,
    fin_q, fin_o, u_q, u_o, full_q, full_o, small_out, state, sums,
    core_q, core_o, acc_q, acc_o, send_q, send_o, plane_q, plane_o,
    quarter_q, quarter_o, zsend_q, zsend_o, zin_q, zin_o,
    fv_q, fv_o, sv_q, sv_o, small_core, small_plane, small_z,
    gn, gb, wn, wb, fn, fb, sn, sb,
    shard_send, shard_recv, plane_send, plane_recv, z_send, z_recv, local, packing,
):
    S, B, A = z.S, z.B, z.A
    s = lax.axis_index("shard")
    r = lax.axis_index("replica")
    a, b = lax.div(r, B), lax.rem(r, B)
    grads, weights, firsts, seconds = (gq, go), (wq, wo), (fq, fo), (sq, so)
    fins, us, fulls = (fin_q, fin_o), (u_q, u_o), (full_q, full_o)
    cores, accs, sends, planes = (core_q, core_o), (acc_q, acc_o), (send_q, send_o), (plane_q, plane_o)
    quarters, zsends, zins = (quarter_q, quarter_o), (zsend_q, zsend_o), (zin_q, zin_o)
    fvs, svs = (fv_q, fv_o), (sv_q, sv_o)
    started = []

    def shard_peer(d):
        return lax.rem(s + d, S)

    def plane_peer(d):
        return (a * B + lax.rem(b + d, B), s)

    def z_peer(d):
        return (lax.rem(a + d, A) * B + b, s)

    def go_to(src, dst, send, recv, device):
        copy = pltpu.make_async_remote_copy(
            src_ref=src, dst_ref=dst, send_sem=send, recv_sem=recv,
            device_id=device, device_id_type=MESH,
        )
        copy.start()
        started.append(copy)
        return copy

    def to_shard(kind, src_of, dst):
        return [
            go_to(src_of(shard_peer(d)), dst, shard_send.at[kind, d], shard_recv.at[kind, d], (r, shard_peer(d)))
            for d in range(1, S)
        ]

    def to_plane(kind, src_of, dst_of):
        return [
            go_to(src_of(lax.rem(b + d, B)), dst_of(d), plane_send.at[kind, d], plane_recv.at[kind, d], plane_peer(d))
            for d in range(1, B)
        ]

    def to_z(kind, src_of, dst_of):
        return [
            go_to(src_of(lax.rem(a + d, A)), dst_of(d), z_send.at[kind, d], z_recv.at[kind, d], z_peer(d))
            for d in range(1, A)
        ]

    def arrived(copies):
        for copy in copies:
            copy.wait_recv()

    def rows(index, count, step):
        return pl.ds(pl.multiple_of(index * count, step), count)

    own = []
    for c in range(2):
        copy = pltpu.make_async_copy(grads[c].at[0, rows(s, z.n[c], 8), :], cores[c].at[s], local.at[c])
        copy.start()
        own.append(copy)

    tiny = []
    for i, (src, dst) in enumerate((
        (gn_h, gn), (gb_h, gb), (wn_h, wn), (wb_h, wb), (fn_h, fn), (fb_h, fb), (sn_h, sn), (sb_h, sb),
    )):
        copy = pltpu.make_async_copy(src, dst, local.at[2 + i])
        copy.start()
        tiny.append(copy)

    barrier = pltpu.get_barrier_semaphore()
    for d in range(1, S):
        pl.semaphore_signal(barrier, inc=1, device_id=(r, shard_peer(d)), device_id_type=MESH)
    for d in range(1, B):
        pl.semaphore_signal(barrier, inc=1, device_id=plane_peer(d), device_id_type=MESH)
    for d in range(1, A):
        pl.semaphore_signal(barrier, inc=1, device_id=z_peer(d), device_id_type=MESH)

    pl.semaphore_wait(barrier, S + B + A - 3)

    core_in = [
        to_shard(c, lambda peer, c=c: grads[c].at[0, rows(peer, z.n[c], 8), :], cores[c].at[s])
        for c in range(2)
    ]

    for copy in tiny:
        copy.wait()
    small_core[s] = jnp.zeros((z.small_rows, LANES), jnp.float32)
    for i in range(z.q * S):
        small_core[s, i : i + 1, : z.L] = gn[:, i * z.L : (i + 1) * z.L]
    for h in range(z.heads):
        small_core[s, z.norm_rows + h : z.norm_rows + h + 1, : z.b * S] = gb[h]
    state[s] = jnp.zeros((z.state_rows, LANES), jnp.float32)
    for t, ref in enumerate((wn, fn, sn)):
        for i in range(z.q):
            row = t * z.q + i
            state[s, row : row + 1, : z.L] = ref[:, i * z.L : (i + 1) * z.L]
    for t, ref in enumerate((wb, fb, sb)):
        row = z.state_norm + t * z.hp
        state[s, row : row + z.heads, : z.b] = ref[...]
    small_in = to_shard(2, lambda peer: small_core.at[s], small_core.at[s])

    held = ([], [])
    for c in range(2):
        n = z.n[c]
        for t, (src, dst) in enumerate(((weights[c], fulls[c].at[s]), (firsts[c], fvs[c]), (seconds[c], svs[c]))):
            for j in range(z.blocks[c]):
                copy = pltpu.make_async_copy(
                    src.at[:, j * LANES : (j + 1) * LANES], dst.at[j * n : (j + 1) * n, :], packing.at[3 * c + t, j]
                )
                copy.start()
                held[t > 0].append(copy)
            if z.used[c] < z.total[c]:
                dst[z.used[c] :, :] = jnp.zeros((z.total[c] - z.used[c], LANES), jnp.float32)

    plane_in = []
    for c in range(2):
        own[c].wait()
        arrived(core_in[c])
        n = z.n[c]
        for j in range(z.blocks[c]):
            part = cores[c][0, :, j * LANES : (j + 1) * LANES]
            for k in range(1, S):
                part = part + cores[c][k, :, j * LANES : (j + 1) * LANES]
            accs[c][j * n : (j + 1) * n, :] = part
            sends[c][j * n : (j + 1) * n, :] = part.astype(jnp.bfloat16)
        if z.used[c] < z.total[c]:
            rest = (z.total[c] - z.used[c], LANES)
            accs[c][z.used[c] :, :] = jnp.zeros(rest, jnp.float32)
            sends[c][z.used[c] :, :] = jnp.zeros(rest, jnp.bfloat16)
        plane_in.append(
            to_plane(
                c,
                lambda peer, c=c: sends[c].at[rows(peer, z.quarter[c], 16), :],
                lambda d, c=c: planes[c].at[d - 1],
            )
        )
    arrived(small_in)
    small = small_core[0]
    for k in range(1, S):
        small = small + small_core[k]
    small_plane[b] = small
    small_in = to_plane(2, lambda peer: small_plane.at[b], lambda d: small_plane.at[b])

    late = []
    for copy in held[0]:
        copy.wait()
    for c in range(2):
        late += to_shard(3 + c, lambda peer, c=c: fulls[c].at[s], fulls[c].at[s])
    late += to_shard(5, lambda peer: state.at[s], state.at[s])

    z_in = []
    for c in range(2):
        arrived(plane_in[c])
        part = accs[c][rows(b, z.quarter[c], 16), :]
        for d in range(1, B):
            part = part + planes[c][d - 1].astype(jnp.float32)
        quarters[c][...] = part
        zsends[c][...] = part.astype(jnp.bfloat16)
        z_in.append(
            to_z(
                c,
                lambda peer, c=c: zsends[c].at[rows(peer, z.piece[c], 16), :],
                lambda d, c=c: zins[c].at[d - 1],
            )
        )
    arrived(small_in)
    small = small_plane[0]
    for k in range(1, B):
        small = small + small_plane[k]
    small_z[a] = small
    small_in = to_z(2, lambda peer: small_z.at[a], lambda d: small_z.at[a])

    back_z = []
    for c in range(2):
        arrived(z_in[c])
        part = quarters[c][rows(a, z.piece[c], 16), :]
        for d in range(1, A):
            part = part + zins[c][d - 1].astype(jnp.float32)
        mine = rows(b * A + a, z.piece[c], 16)
        fins[c][mine, :] = part.astype(jnp.bfloat16)
        back_z.append(
            to_z(3 + c, lambda peer, c=c, mine=mine: fins[c].at[mine, :], lambda d, c=c, mine=mine: fins[c].at[mine, :])
        )

    back_plane = []
    for c in range(2):
        arrived(back_z[c])
        mine = rows(b, z.quarter[c], 16)
        back_plane.append(
            to_plane(3 + c, lambda peer, c=c, mine=mine: fins[c].at[mine, :], lambda d, c=c, mine=mine: fins[c].at[mine, :])
        )
    for copy in held[1]:
        copy.wait()
    sums[s] = jnp.zeros((z.sum_rows, LANES), jnp.float32)
    for c in range(2):
        weight = fulls[c][s]
        sums[s, c * (B + 1) : c * (B + 1) + 1, :] = jnp.sum(weight * weight, axis=0, keepdims=True)

    def updates(c, d):
        index = lax.rem(b + B - d, B)
        mine = rows(index, z.quarter[c], 16)
        summed = fins[c][mine, :].astype(jnp.float32)
        _, _, update = step_math(summed, fvs[c][mine, :], svs[c][mine, :])
        update = update + DECAY * fulls[c][s, mine, :]
        sums[s, pl.ds(c * (B + 1) + 1 + index, 1), :] = jnp.sum(update * update, axis=0, keepdims=True)
        us[c][s, mine, :] = update.astype(jnp.bfloat16)
        return to_shard(
            6 + c * B + d, lambda peer: us[c].at[s, mine, :], us[c].at[s, mine, :]
        )

    for c in range(2):
        late += updates(c, 0)
    arrived(small_in)
    small = small_z[0]
    for k in range(1, A):
        small = small + small_z[k]
    small_out[...] = small
    for c in range(2):
        for d in range(1, B):
            back_plane[c][d - 1].wait_recv()
            late += updates(c, d)
    late += to_shard(6 + 2 * B, lambda peer: sums.at[s], sums.at[s])
    arrived(late)
    for copy in started:
        copy.wait_send()


def finish_kernel(
    z,
    fin_q, fin_o, u_q, u_o, full_q, full_o, small, state, sums, fq, fo, sq, so,
    new_q, new_o, new_n, new_b, fq_next, fo_next, fn_next, fb_next,
    sq_next, so_next, sn_next, sb_next, table, trust,
):
    S, L, h = z.S, z.L, z.heads
    s = lax.axis_index("shard")
    totals = sums[0]
    for k in range(1, S):
        totals = totals + sums[k]

    def whole(row, count):
        value = totals[row : row + 1, :]
        for i in range(1, count):
            value = value + totals[row + i : row + i + 1, :]
        return jnp.sum(value, axis=1, keepdims=True)

    squares = [(whole(c * (z.B + 1), 1), whole(c * (z.B + 1) + 1, z.B)) for c in range(2)]

    def norm_of(k):
        rows = [state[k, t * z.q : (t + 1) * z.q, :L] for t in range(3)]
        return small[pl.ds(k * z.q, z.q), :L], rows

    def bias_of(k):
        rows = [state[k, z.state_norm + t * z.hp : z.state_norm + t * z.hp + h, : z.b] for t in range(3)]
        return small[z.norm_rows : z.norm_rows + h, k * z.b : (k + 1) * z.b], rows

    def total(value):
        return jnp.sum(jnp.sum(value, axis=0, keepdims=True), axis=1, keepdims=True)

    pairs = []
    for part_of in (norm_of, bias_of):
        couples, wsum, usum = [], None, None
        for k in range(S):
            summed, (weight, moment, second) = part_of(k)
            update = step_math(summed, moment, second)[2]
            couples.append((weight, update))
            ws, us = total(weight * weight), total(update * update)
            wsum = ws if wsum is None else wsum + ws
            usum = us if usum is None else usum + us
        squares.append((wsum, usum))
        pairs.append(couples)

    wsizes = [jnp.sqrt(pair[0]) for pair in squares]
    usizes = [jnp.sqrt(pair[1]) for pair in squares]
    ratios = [w / (u + 1e-06) for w, u in zip(wsizes, usizes)]

    column = lax.broadcasted_iota(jnp.int32, (2, 4), 1)
    row = lax.broadcasted_iota(jnp.int32, (2, 4), 0)
    values = jnp.zeros((2, 4), jnp.float32)
    for k in range(4):
        values = jnp.where(column == k, jnp.where(row == 0, wsizes[k], usizes[k]), values)
    table[...] = values
    column = lax.broadcasted_iota(jnp.int32, (1, 4), 1)
    values = jnp.zeros((1, 4), jnp.float32)
    for k in range(4):
        values = jnp.where(column == k, ratios[k], values)
    trust[...] = values

    for k in range(S):
        weight, update = pairs[0][k]
        value = (weight - 0.01 * ratios[2] * update).astype(jnp.bfloat16)
        for i in range(z.q):
            at = (k * z.q + i) * L
            new_n[at : at + L] = value[i]
        weight, update = pairs[1][k]
        new_b[:, k * z.b : (k + 1) * z.b] = (weight - 0.01 * ratios[3] * update).astype(jnp.bfloat16)
    summed, (_, moment, second) = norm_of(s)
    moment_next, second_next, _ = step_math(summed, moment, second)
    for i in range(z.q):
        fn_next[:, i * L : (i + 1) * L] = moment_next[i : i + 1, :]
        sn_next[:, i * L : (i + 1) * L] = second_next[i : i + 1, :]
    moment_next = second_next = jnp.zeros((h, z.b), jnp.float32)
    for k in range(S):
        summed, (_, moment, second) = bias_of(k)
        moment_value, second_value, _ = step_math(summed, moment, second)
        moment_next = jnp.where(s == k, moment_value, moment_next)
        second_next = jnp.where(s == k, second_value, second_next)
    fb_next[...] = moment_next
    sb_next[...] = second_next

    for c, (fin, u, full, first, second, new, first_next, second_next) in enumerate((
        (fin_q, u_q, full_q, fq, sq, new_q, fq_next, sq_next),
        (fin_o, u_o, full_o, fo, so, new_o, fo_next, so_next),
    )):
        n = z.n[c]
        for j in range(z.blocks[c]):
            lanes = slice(j * LANES, (j + 1) * LANES)
            summed = fin[j * n : (j + 1) * n, :].astype(jnp.float32)
            moment_value, second_value, _ = step_math(summed, first[:, lanes], second[:, lanes])
            first_next[:, lanes] = moment_value
            second_next[:, lanes] = second_value
            for k in range(S):
                own = slice(k * n, (k + 1) * n)
                update = u[k, j * n : (j + 1) * n, :].astype(jnp.float32)
                new[own, lanes] = (full[k, j * n : (j + 1) * n, :] - 0.01 * ratios[c] * update).astype(jnp.bfloat16)


def on_device(
    shards, replicas,
    gq, go, gn, gb, wq, wo, wn, wb, fq, fo, fn, fb, sq, so, sn, sb,
):
    f32, bf16 = jnp.float32, jnp.bfloat16
    wb, fb, sb = (value.T for value in (wb, fb, sb))
    gb = jnp.transpose(gb, (2, 0, 1))
    z = Sizes(shards, replicas, wq.shape, wo.shape, wn.shape, wb.shape)
    S, B, A = z.S, z.B, z.A
    wn, fn, sn = (value.reshape(1, -1) for value in (wn, fn, sn))
    vmem = pl.BlockSpec(memory_space=pltpu.VMEM)
    shape = jax.ShapeDtypeStruct
    whole = [(n * S, cols) for n, cols in zip(z.n, z.cols)]
    both = (0, 1)

    def scratch(shape_of, dtype):
        return [pltpu.VMEM(shape_of(c), dtype) for c in both]

    outs = pl.pallas_call(
        functools.partial(exchange_kernel, z),
        out_shape=[shape((z.total[c], LANES), bf16) for c in both]
        + [shape((S, z.total[c], LANES), bf16) for c in both]
        + [shape((S, z.total[c], LANES), f32) for c in both]
        + [shape((z.small_rows, LANES), f32), shape((S, z.state_rows, LANES), f32), shape((S, z.sum_rows, LANES), f32)],
        in_specs=[pl.BlockSpec(memory_space=pltpu.HBM)] * 16,
        out_specs=[vmem] * 9,
        scratch_shapes=scratch(lambda c: (S, z.n[c], z.cols[c]), f32)
        + scratch(lambda c: (z.total[c], LANES), f32)
        + scratch(lambda c: (z.total[c], LANES), bf16)
        + scratch(lambda c: (max(B - 1, 1), z.quarter[c], LANES), bf16)
        + scratch(lambda c: (z.quarter[c], LANES), f32)
        + scratch(lambda c: (z.quarter[c], LANES), bf16)
        + scratch(lambda c: (max(A - 1, 1), z.piece[c], LANES), bf16)
        + scratch(lambda c: (z.total[c], LANES), f32) * 2
        + [pltpu.VMEM((k, z.small_rows, LANES), f32) for k in (S, B, A)]
        + [pltpu.VMEM(value.shape, f32) for value in (gn, gb, wn, wb, fn, fb, sn, sb)]
        + [pltpu.SemaphoreType.DMA((7 + 2 * B, S))] * 2
        + [pltpu.SemaphoreType.DMA((5, B))] * 2
        + [pltpu.SemaphoreType.DMA((5, A))] * 2
        + [pltpu.SemaphoreType.DMA((12,)), pltpu.SemaphoreType.DMA((6, max(z.blocks)))],
        compiler_params=pltpu.CompilerParams(
            collective_id=0, has_side_effects=True, vmem_limit_bytes=60 * 1024 * 1024
        ),
        name="exchange",
    )(gq, go, gn, gb, wq, wo, wn, wb, fq, fo, fn, fb, sq, so, sn, sb)

    results = pl.pallas_call(
        functools.partial(finish_kernel, z),
        out_shape=[
            shape(whole[0], bf16), shape(whole[1], bf16),
            shape((wn.shape[1] * S,), bf16), shape((z.heads, z.b * S), bf16),
        ]
        + [shape(ref.shape, f32) for ref in (fq, fo, fn, fb)] * 2
        + [shape((2, 4), f32), shape((1, 4), f32)],
        in_specs=[vmem] * 13,
        out_specs=[vmem] * 14,
        compiler_params=pltpu.CompilerParams(vmem_limit_bytes=60 * 1024 * 1024),
        name="finish",
    )(*outs, fq, fo, sq, so)
    results = list(results)
    for at in (6, 10, 13):
        results[at] = results[at].reshape(-1)
    for at in (3, 7, 11):
        results[at] = results[at].T
    return tuple(results)


def solution(mesh):
    shards, replicas = mesh.shape["shard"], mesh.shape["replica"]
    every = ("replica", "shard")
    state = (P("shard", None), P("shard", None), P("shard"), P("shard", None))
    return jax.shard_map(
        functools.partial(on_device, shards, replicas),
        mesh=mesh,
        in_specs=(P(every, None, None), P(every, None, None), P(every, None), P(every, None, None)) + state * 3,
        out_specs=(P(), P(), P(), P()) + state * 2 + (P(), P()),
        check_vma=False,
    )
```

```python
import functools

import jax
import jax.numpy as jnp
from jax import lax
from jax.experimental import pallas as pl
from jax.experimental.pallas import tpu as pltpu
from jax.sharding import PartitionSpec as P

MESH = pl.DeviceIdType.MESH
LANES = 128
DECAY = 0.01


def up(value, step):
    return -(-value // step) * step


class Sizes:
    def __init__(self, shards, replicas, query, output, norm, bias):
        self.S, self.R = shards, replicas
        self.B = 4 if replicas % 4 == 0 else 1
        self.A = replicas // self.B
        self.n = (query[0], output[0])
        self.cols = (query[1], output[1])
        self.blocks = tuple(c // LANES for c in self.cols)
        self.used = tuple(n * j for n, j in zip(self.n, self.blocks))
        self.piece = tuple(up(-(-u // replicas), 16) for u in self.used)
        self.quarter = tuple(self.A * p for p in self.piece)
        self.total = tuple(replicas * p for p in self.piece)
        self.L = min(LANES, norm[0])
        self.q = norm[0] // self.L
        self.norm_rows = up(self.q * shards, 8)
        self.heads, self.b = bias
        self.hp = up(self.heads, 8)
        self.small_rows = self.norm_rows + self.hp
        self.state_norm = up(3 * self.q, 8)
        self.state_rows = self.state_norm + 3 * self.hp
        self.sum_rows = up(2 * (self.B + 1), 8)


def step_math(summed, moment, second):
    moment_next = 0.5 * moment + 0.5 * summed
    second_next = 0.5 * second + 0.5 * summed * summed
    return moment_next, second_next, moment_next / (jnp.sqrt(second_next) + 1e-06)


def exchange_kernel(
    z,
    gq, go, gn_h, gb_h, wq, wo, wn_h, wb_h, fq, fo, fn_h, fb_h, sq, so, sn_h, sb_h,
    fin_q, fin_o, u_q, u_o, full_q, full_o, small_out, state, sums,
    core_q, core_o, acc_q, acc_o, send_q, send_o, plane_q, plane_o,
    quarter_q, quarter_o, zsend_q, zsend_o, zin_q, zin_o,
    fv_q, fv_o, sv_q, sv_o, small_core, small_plane, small_z,
    gn, gb, wn, wb, fn, fb, sn, sb,
    shard_send, shard_recv, plane_send, plane_recv, z_send, z_recv, local, packing,
):
    S, B, A = z.S, z.B, z.A
    s = lax.axis_index("shard")
    r = lax.axis_index("replica")
    a, b = lax.div(r, B), lax.rem(r, B)
    grads, weights, firsts, seconds = (gq, go), (wq, wo), (fq, fo), (sq, so)
    fins, us, fulls = (fin_q, fin_o), (u_q, u_o), (full_q, full_o)
    cores, accs, sends, planes = (core_q, core_o), (acc_q, acc_o), (send_q, send_o), (plane_q, plane_o)
    quarters, zsends, zins = (quarter_q, quarter_o), (zsend_q, zsend_o), (zin_q, zin_o)
    fvs, svs = (fv_q, fv_o), (sv_q, sv_o)
    started = []

    def shard_peer(d):
        return lax.rem(s + d, S)

    def plane_peer(d):
        return (a * B + lax.rem(b + d, B), s)

    def z_peer(d):
        return (lax.rem(a + d, A) * B + b, s)

    def go_to(src, dst, send, recv, device):
        copy = pltpu.make_async_remote_copy(
            src_ref=src, dst_ref=dst, send_sem=send, recv_sem=recv,
            device_id=device, device_id_type=MESH,
        )
        copy.start()
        started.append(copy)
        return copy

    def to_shard(kind, src_of, dst):
        return [
            go_to(src_of(shard_peer(d)), dst, shard_send.at[kind, d], shard_recv.at[kind, d], (r, shard_peer(d)))
            for d in range(1, S)
        ]

    def to_plane(kind, src_of, dst_of):
        return [
            go_to(src_of(lax.rem(b + d, B)), dst_of(d), plane_send.at[kind, d], plane_recv.at[kind, d], plane_peer(d))
            for d in range(1, B)
        ]

    def to_z(kind, src_of, dst_of):
        return [
            go_to(src_of(lax.rem(a + d, A)), dst_of(d), z_send.at[kind, d], z_recv.at[kind, d], z_peer(d))
            for d in range(1, A)
        ]

    def arrived(copies):
        for copy in copies:
            copy.wait_recv()

    def rows(index, count, step):
        return pl.ds(pl.multiple_of(index * count, step), count)

    own = []
    for c in range(2):
        copy = pltpu.make_async_copy(grads[c].at[0, rows(s, z.n[c], 8), :], cores[c].at[s], local.at[c])
        copy.start()
        own.append(copy)

    tiny = []
    for i, (src, dst) in enumerate((
        (gn_h, gn), (gb_h, gb), (wn_h, wn), (wb_h, wb), (fn_h, fn), (fb_h, fb), (sn_h, sn), (sb_h, sb),
    )):
        copy = pltpu.make_async_copy(src, dst, local.at[2 + i])
        copy.start()
        tiny.append(copy)

    barrier = pltpu.get_barrier_semaphore()
    for d in range(1, S):
        pl.semaphore_signal(barrier, inc=1, device_id=(r, shard_peer(d)), device_id_type=MESH)
    for d in range(1, B):
        pl.semaphore_signal(barrier, inc=1, device_id=plane_peer(d), device_id_type=MESH)
    for d in range(1, A):
        pl.semaphore_signal(barrier, inc=1, device_id=z_peer(d), device_id_type=MESH)

    pl.semaphore_wait(barrier, S + B + A - 3)

    core_in = [
        to_shard(c, lambda peer, c=c: grads[c].at[0, rows(peer, z.n[c], 8), :], cores[c].at[s])
        for c in range(2)
    ]

    for copy in tiny:
        copy.wait()
    small_core[s] = jnp.zeros((z.small_rows, LANES), jnp.float32)
    for i in range(z.q * S):
        small_core[s, i : i + 1, : z.L] = gn[:, i * z.L : (i + 1) * z.L]
    for h in range(z.heads):
        small_core[s, z.norm_rows + h : z.norm_rows + h + 1, : z.b * S] = gb[h]
    state[s] = jnp.zeros((z.state_rows, LANES), jnp.float32)
    for t, ref in enumerate((wn, fn, sn)):
        for i in range(z.q):
            row = t * z.q + i
            state[s, row : row + 1, : z.L] = ref[:, i * z.L : (i + 1) * z.L]
    for t, ref in enumerate((wb, fb, sb)):
        row = z.state_norm + t * z.hp
        state[s, row : row + z.heads, : z.b] = ref[...]
    small_in = to_shard(2, lambda peer: small_core.at[s], small_core.at[s])

    held = ([], [])
    for c in range(2):
        n = z.n[c]
        for t, (src, dst) in enumerate(((weights[c], fulls[c].at[s]), (firsts[c], fvs[c]), (seconds[c], svs[c]))):
            for j in range(z.blocks[c]):
                copy = pltpu.make_async_copy(
                    src.at[:, j * LANES : (j + 1) * LANES], dst.at[j * n : (j + 1) * n, :], packing.at[3 * c + t, j]
                )
                copy.start()
                held[t > 0].append(copy)
            if z.used[c] < z.total[c]:
                dst[z.used[c] :, :] = jnp.zeros((z.total[c] - z.used[c], LANES), jnp.float32)

    plane_in = []
    for c in range(2):
        own[c].wait()
        arrived(core_in[c])
        n = z.n[c]
        for j in range(z.blocks[c]):
            part = cores[c][0, :, j * LANES : (j + 1) * LANES]
            for k in range(1, S):
                part = part + cores[c][k, :, j * LANES : (j + 1) * LANES]
            accs[c][j * n : (j + 1) * n, :] = part
            sends[c][j * n : (j + 1) * n, :] = part.astype(jnp.bfloat16)
        if z.used[c] < z.total[c]:
            rest = (z.total[c] - z.used[c], LANES)
            accs[c][z.used[c] :, :] = jnp.zeros(rest, jnp.float32)
            sends[c][z.used[c] :, :] = jnp.zeros(rest, jnp.bfloat16)
        plane_in.append(
            to_plane(
                c,
                lambda peer, c=c: sends[c].at[rows(peer, z.quarter[c], 16), :],
                lambda d, c=c: planes[c].at[d - 1],
            )
        )
    arrived(small_in)
    small = small_core[0]
    for k in range(1, S):
        small = small + small_core[k]
    small_plane[b] = small
    small_in = to_plane(2, lambda peer: small_plane.at[b], lambda d: small_plane.at[b])

    late = []
    for copy in held[0]:
        copy.wait()
    for c in range(2):
        late += to_shard(3 + c, lambda peer, c=c: fulls[c].at[s], fulls[c].at[s])
    late += to_shard(5, lambda peer: state.at[s], state.at[s])

    z_in = []
    for c in range(2):
        arrived(plane_in[c])
        part = accs[c][rows(b, z.quarter[c], 16), :]
        for d in range(1, B):
            part = part + planes[c][d - 1].astype(jnp.float32)
        quarters[c][...] = part
        zsends[c][...] = part.astype(jnp.bfloat16)
        z_in.append(
            to_z(
                c,
                lambda peer, c=c: zsends[c].at[rows(peer, z.piece[c], 16), :],
                lambda d, c=c: zins[c].at[d - 1],
            )
        )
    arrived(small_in)
    small = small_plane[0]
    for k in range(1, B):
        small = small + small_plane[k]
    small_z[a] = small
    small_in = to_z(2, lambda peer: small_z.at[a], lambda d: small_z.at[a])

    back_z = []
    back_plane = [[], []]

    def forward(c, d):
        piece = rows(b * A + lax.rem(a + A - d, A), z.piece[c], 16)
        back_plane[c].append(
            to_plane(3 + c * A + d, lambda peer: fins[c].at[piece, :], lambda offset: fins[c].at[piece, :])
        )

    for c in range(2):
        arrived(z_in[c])
        part = quarters[c][rows(a, z.piece[c], 16), :]
        for d in range(1, A):
            part = part + zins[c][d - 1].astype(jnp.float32)
        mine = rows(b * A + a, z.piece[c], 16)
        fins[c][mine, :] = part.astype(jnp.bfloat16)
        back_z.append(
            to_z(3 + c, lambda peer, c=c, mine=mine: fins[c].at[mine, :], lambda d, c=c, mine=mine: fins[c].at[mine, :])
        )

        forward(c, 0)

    for c in range(2):
        for d in range(1, A):
            back_z[c][d - 1].wait_recv()
            forward(c, d)
    for copy in held[1]:
        copy.wait()
    sums[s] = jnp.zeros((z.sum_rows, LANES), jnp.float32)
    for c in range(2):
        weight = fulls[c][s]
        sums[s, c * (B + 1) : c * (B + 1) + 1, :] = jnp.sum(weight * weight, axis=0, keepdims=True)

    def updates(c, d):
        index = lax.rem(b + B - d, B)
        mine = rows(index, z.quarter[c], 16)
        summed = fins[c][mine, :].astype(jnp.float32)
        _, _, update = step_math(summed, fvs[c][mine, :], svs[c][mine, :])
        update = update + DECAY * fulls[c][s, mine, :]
        sums[s, pl.ds(c * (B + 1) + 1 + index, 1), :] = jnp.sum(update * update, axis=0, keepdims=True)
        us[c][s, mine, :] = update.astype(jnp.bfloat16)
        return to_shard(
            6 + c * B + d, lambda peer: us[c].at[s, mine, :], us[c].at[s, mine, :]
        )

    for c in range(2):
        late += updates(c, 0)
    arrived(small_in)
    small = small_z[0]
    for k in range(1, A):
        small = small + small_z[k]
    small_out[...] = small
    for c in range(2):
        for d in range(1, B):
            for copies in back_plane[c]:
                copies[d - 1].wait_recv()
            late += updates(c, d)
    late += to_shard(6 + 2 * B, lambda peer: sums.at[s], sums.at[s])
    arrived(late)
    for copy in started:
        copy.wait_send()


def finish_kernel(
    z,
    fin_q, fin_o, u_q, u_o, full_q, full_o, small, state, sums, fq, fo, sq, so,
    new_q, new_o, new_n, new_b, fq_next, fo_next, fn_next, fb_next,
    sq_next, so_next, sn_next, sb_next, table, trust,
):
    S, L, h = z.S, z.L, z.heads
    s = lax.axis_index("shard")
    totals = sums[0]
    for k in range(1, S):
        totals = totals + sums[k]

    def whole(row, count):
        value = totals[row : row + 1, :]
        for i in range(1, count):
            value = value + totals[row + i : row + i + 1, :]
        return jnp.sum(value, axis=1, keepdims=True)

    squares = [(whole(c * (z.B + 1), 1), whole(c * (z.B + 1) + 1, z.B)) for c in range(2)]

    def norm_of(k):
        rows = [state[k, t * z.q : (t + 1) * z.q, :L] for t in range(3)]
        return small[pl.ds(k * z.q, z.q), :L], rows

    def bias_of(k):
        rows = [state[k, z.state_norm + t * z.hp : z.state_norm + t * z.hp + h, : z.b] for t in range(3)]
        return small[z.norm_rows : z.norm_rows + h, k * z.b : (k + 1) * z.b], rows

    def total(value):
        return jnp.sum(jnp.sum(value, axis=0, keepdims=True), axis=1, keepdims=True)

    pairs = []
    for part_of in (norm_of, bias_of):
        couples, wsum, usum = [], None, None
        for k in range(S):
            summed, (weight, moment, second) = part_of(k)
            update = step_math(summed, moment, second)[2]
            couples.append((weight, update))
            ws, us = total(weight * weight), total(update * update)
            wsum = ws if wsum is None else wsum + ws
            usum = us if usum is None else usum + us
        squares.append((wsum, usum))
        pairs.append(couples)

    wsizes = [jnp.sqrt(pair[0]) for pair in squares]
    usizes = [jnp.sqrt(pair[1]) for pair in squares]
    ratios = [w / (u + 1e-06) for w, u in zip(wsizes, usizes)]

    column = lax.broadcasted_iota(jnp.int32, (2, 4), 1)
    row = lax.broadcasted_iota(jnp.int32, (2, 4), 0)
    values = jnp.zeros((2, 4), jnp.float32)
    for k in range(4):
        values = jnp.where(column == k, jnp.where(row == 0, wsizes[k], usizes[k]), values)
    table[...] = values
    column = lax.broadcasted_iota(jnp.int32, (1, 4), 1)
    values = jnp.zeros((1, 4), jnp.float32)
    for k in range(4):
        values = jnp.where(column == k, ratios[k], values)
    trust[...] = values

    for k in range(S):
        weight, update = pairs[0][k]
        value = (weight - 0.01 * ratios[2] * update).astype(jnp.bfloat16)
        for i in range(z.q):
            at = (k * z.q + i) * L
            new_n[at : at + L] = value[i]
        weight, update = pairs[1][k]
        new_b[:, k * z.b : (k + 1) * z.b] = (weight - 0.01 * ratios[3] * update).astype(jnp.bfloat16)
    summed, (_, moment, second) = norm_of(s)
    moment_next, second_next, _ = step_math(summed, moment, second)
    for i in range(z.q):
        fn_next[:, i * L : (i + 1) * L] = moment_next[i : i + 1, :]
        sn_next[:, i * L : (i + 1) * L] = second_next[i : i + 1, :]
    moment_next = second_next = jnp.zeros((h, z.b), jnp.float32)
    for k in range(S):
        summed, (_, moment, second) = bias_of(k)
        moment_value, second_value, _ = step_math(summed, moment, second)
        moment_next = jnp.where(s == k, moment_value, moment_next)
        second_next = jnp.where(s == k, second_value, second_next)
    fb_next[...] = moment_next
    sb_next[...] = second_next

    for c, (fin, u, full, first, second, new, first_next, second_next) in enumerate((
        (fin_q, u_q, full_q, fq, sq, new_q, fq_next, sq_next),
        (fin_o, u_o, full_o, fo, so, new_o, fo_next, so_next),
    )):
        n = z.n[c]
        for j in range(z.blocks[c]):
            lanes = slice(j * LANES, (j + 1) * LANES)
            summed = fin[j * n : (j + 1) * n, :].astype(jnp.float32)
            moment_value, second_value, _ = step_math(summed, first[:, lanes], second[:, lanes])
            first_next[:, lanes] = moment_value
            second_next[:, lanes] = second_value
            for k in range(S):
                own = slice(k * n, (k + 1) * n)
                update = u[k, j * n : (j + 1) * n, :].astype(jnp.float32)
                new[own, lanes] = (full[k, j * n : (j + 1) * n, :] - 0.01 * ratios[c] * update).astype(jnp.bfloat16)


def on_device(
    shards, replicas,
    gq, go, gn, gb, wq, wo, wn, wb, fq, fo, fn, fb, sq, so, sn, sb,
):
    f32, bf16 = jnp.float32, jnp.bfloat16
    wb, fb, sb = (value.T for value in (wb, fb, sb))
    gb = jnp.transpose(gb, (2, 0, 1))
    z = Sizes(shards, replicas, wq.shape, wo.shape, wn.shape, wb.shape)
    S, B, A = z.S, z.B, z.A
    wn, fn, sn = (value.reshape(1, -1) for value in (wn, fn, sn))
    vmem = pl.BlockSpec(memory_space=pltpu.VMEM)
    shape = jax.ShapeDtypeStruct
    whole = [(n * S, cols) for n, cols in zip(z.n, z.cols)]
    both = (0, 1)

    def scratch(shape_of, dtype):
        return [pltpu.VMEM(shape_of(c), dtype) for c in both]

    outs = pl.pallas_call(
        functools.partial(exchange_kernel, z),
        out_shape=[shape((z.total[c], LANES), bf16) for c in both]
        + [shape((S, z.total[c], LANES), bf16) for c in both]
        + [shape((S, z.total[c], LANES), f32) for c in both]
        + [shape((z.small_rows, LANES), f32), shape((S, z.state_rows, LANES), f32), shape((S, z.sum_rows, LANES), f32)],
        in_specs=[pl.BlockSpec(memory_space=pltpu.HBM)] * 16,
        out_specs=[vmem] * 9,
        scratch_shapes=scratch(lambda c: (S, z.n[c], z.cols[c]), f32)
        + scratch(lambda c: (z.total[c], LANES), f32)
        + scratch(lambda c: (z.total[c], LANES), bf16)
        + scratch(lambda c: (max(B - 1, 1), z.quarter[c], LANES), bf16)
        + scratch(lambda c: (z.quarter[c], LANES), f32)
        + scratch(lambda c: (z.quarter[c], LANES), bf16)
        + scratch(lambda c: (max(A - 1, 1), z.piece[c], LANES), bf16)
        + scratch(lambda c: (z.total[c], LANES), f32) * 2
        + [pltpu.VMEM((k, z.small_rows, LANES), f32) for k in (S, B, A)]
        + [pltpu.VMEM(value.shape, f32) for value in (gn, gb, wn, wb, fn, fb, sn, sb)]
        + [pltpu.SemaphoreType.DMA((7 + 2 * B, S))] * 2
        + [pltpu.SemaphoreType.DMA((3 + 2 * A, B))] * 2
        + [pltpu.SemaphoreType.DMA((5, A))] * 2
        + [pltpu.SemaphoreType.DMA((12,)), pltpu.SemaphoreType.DMA((6, max(z.blocks)))],
        compiler_params=pltpu.CompilerParams(
            collective_id=0, has_side_effects=True, vmem_limit_bytes=60 * 1024 * 1024
        ),
        name="exchange",
    )(gq, go, gn, gb, wq, wo, wn, wb, fq, fo, fn, fb, sq, so, sn, sb)

    results = pl.pallas_call(
        functools.partial(finish_kernel, z),
        out_shape=[
            shape(whole[0], bf16), shape(whole[1], bf16),
            shape((wn.shape[1] * S,), bf16), shape((z.heads, z.b * S), bf16),
        ]
        + [shape(ref.shape, f32) for ref in (fq, fo, fn, fb)] * 2
        + [shape((2, 4), f32), shape((1, 4), f32)],
        in_specs=[vmem] * 13,
        out_specs=[vmem] * 14,
        compiler_params=pltpu.CompilerParams(vmem_limit_bytes=60 * 1024 * 1024),
        name="finish",
    )(*outs, fq, fo, sq, so)
    results = list(results)
    for at in (6, 10, 13):
        results[at] = results[at].reshape(-1)
    for at in (3, 7, 11):
        results[at] = results[at].T
    return tuple(results)


def solution(mesh):
    shards, replicas = mesh.shape["shard"], mesh.shape["replica"]
    every = ("replica", "shard")
    state = (P("shard", None), P("shard", None), P("shard"), P("shard", None))
    return jax.shard_map(
        functools.partial(on_device, shards, replicas),
        mesh=mesh,
        in_specs=(P(every, None, None), P(every, None, None), P(every, None), P(every, None, None)) + state * 3,
        out_specs=(P(), P(), P(), P()) + state * 2 + (P(), P()),
        check_vma=False,
    )
```
